32 devices in a mesh: shard: 4 (over z), context: 4 (over x, core), tensor: 2 (over y).
Axes of the slice: x: 2, y: 2, z: 4, core: 2. Of those that a mesh axis runs over, the one named last changes fastest.
Arguments:
- inputs: float32 [4, 512, 1024], P('shard', 'context'), may hold values from -8.5 to 8.5
- attn_gain: bfloat16 [1024], P(('shard', 'context')), may hold values from 0.5 to 1.5
- query_weight: bfloat16 [1024, 1024], P(('shard', 'context'), 'tensor'), may hold values from -0.1875 to 0.1875
- key_weight: bfloat16 [1024, 512], P(('shard', 'context'), 'tensor'), may hold values from -0.1875 to 0.1875
- value_matrix: bfloat16 [1024, 512], P(('shard', 'context'), 'tensor'), may hold values from -0.1875 to 0.1875
- output_weight: bfloat16 [1024, 1024], P(('shard', 'context'), 'tensor'), may hold values from -4 to 4
- ffn_gain: bfloat16 [1024], P(('shard', 'context')), may hold values from 0.5 to 1.5
- gate_weight: bfloat16 [1024, 16, 512], P(('shard', 'context'), None, 'tensor'), may hold values from -0.1875 to 0.1875
- up_weight: bfloat16 [1024, 16, 512], P(('shard', 'context'), None, 'tensor'), may hold values from -0.1875 to 0.1875
- down_weight: bfloat16 [1024, 16, 512], P(('shard', 'context'), None, 'tensor'), may hold values from -2 to 2
- routes: int32 [4, 512, 8], P('shard', 'context'), may hold values from 0 to 15, all different within a row; in each aligned block of 128 rows (0 to 127, 128 to 255, ..., all dimensions but the last counted through in order) at most 80 rows name the same one
- route_weights: float32 [4, 512, 8], P('shard', 'context'), may hold values from 0.05 to 0.25
- cotangent: float32 [4, 512, 1024], P('shard', 'context'), may hold values from -6 to 6
Outputs:
- output: float32 [4, 512, 1024], P('shard', 'context')
- grad_input: float32 [4, 512, 1024], P('shard', 'context')
- grad_attn_gain: float32 [1024], P(('shard', 'context'))
- grad_query_weight: float32 [1024, 1024], P(('shard', 'context'), 'tensor')
- grad_key_weight: float32 [1024, 512], P(('shard', 'context'), 'tensor')
- grad_value_weight: float32 [1024, 512], P(('shard', 'context'), 'tensor')
- grad_output_weight: float32 [1024, 1024], P(('shard', 'context'), 'tensor')
- grad_ffn_gain: float32 [1024], P(('shard', 'context'))
- grad_gate_weight: float32 [1024, 16, 512], P(('shard', 'context'), None, 'tensor')
- grad_up_weight: float32 [1024, 16, 512], P(('shard', 'context'), None, 'tensor')
- grad_down_weight: float32 [1024, 16, 512], P(('shard', 'context'), None, 'tensor')
The draws below stay inside these ranges and needn't reach their ends.
Inputs may be any that keep to these rules, and one draw needn't show every extreme that they name: `routes`: each token names 8 different experts. Within each aligned block of 128 positions of a sequence no expert is named more than 80 times, and some block names some expert exactly 80 times.
All inputs are finite; a program needn't handle non-finite values.
Results may differ from the reference program's by a relative error of at most 0.012.
Values may be sent and summed in bfloat16 or wider, within the bound.
A program may use at most 128 MiB of HBM per device.

```python
import math
import jax
import jax.numpy as jnp
import numpy as np
from jax import lax

MODEL_DIM = 1024
QUERY_HEADS = 16
KEY_VALUE_HEADS = 8
HEAD_DIM = 64
EXPERT_COUNT = 16
EXPERT_HIDDEN = 512
TOP = 8
TOK_DEV = 128
SEQUENCE_LENGTH = 512
SEQS = 4
CAP = 80
N_CONTEXT = 4


def draw_inputs(key, part):
    residual_flow = jax.random.fold_in(key, 11)
    first = jax.random.fold_in(residual_flow, 0)
    return jnp.clip(jax.random.normal(first, (SEQS, SEQUENCE_LENGTH, MODEL_DIM), jnp.float32), -6.0, 6.0)


def with_spikes(array, own_key, source, target, blocks, factor):
    owner, partner = [(jnp.arange(array.shape[position]) // (array.shape[position] // blocks)).reshape([-1 if axis == position else 1 for axis in range(array.ndim)]) for position in (source, target)]
    chosen = jax.random.permutation(own_key, blocks)[partner]
    strong = (owner == chosen) | (owner == (partner + blocks // 2) % blocks)
    return jnp.where(strong, factor * array, array)


def shard_levels(rng, shape, shards, least, high):
    def one(axis_at, shards_of):
        steps = jax.random.uniform(jax.random.fold_in(jax.random.fold_in(rng, 6), axis_at), (shards_of,), jnp.float32, least / len(shards), high / len(shards))
        return jnp.repeat(jnp.exp(steps), shape[axis_at] // shards_of).reshape((-1,) + (1,) * (len(shape) - axis_at - 1))

    loudness = one(*shards[0])
    for cut in shards[1:]:
        loudness = loudness * one(*cut)
    return loudness


def routed_block(key, own, number, rows, amount, top, limit, lean):
    ranking = jax.random.permutation(key, amount)
    packed, usual = shares(amount, rows * top, limit, lean, True), shares(amount, rows * top, limit, lean, False)
    places = jnp.arange(amount)

    def named(lengths, rotation):
        used = int((lengths > 0).sum())
        fixed = max(1, used // 4)
        moved = fixed + (places - fixed + rotation * (used - fixed)) % max(1, amount - fixed)
        return jnp.zeros((amount,), jnp.int32).at[ranking[jnp.where(places < fixed, places, moved)]].set(jnp.asarray(lengths, jnp.int32))

    lengths = jnp.where(number % 4 == 0, named(packed, number // 4), named(usual, number - number // 4 - 1))
    mixed = jax.random.permutation(jax.random.fold_in(own, 3), amount)
    source_of, receiver = mixed[0:amount // 2 * 2:2], mixed[1:amount // 2 * 2:2]
    room = jnp.minimum(lengths[source_of] - 1, limit - lengths[receiver]) // 2
    room = jnp.where((source_of == ranking[0]) | (receiver == ranking[0]) | (lengths[receiver] == 0), 0, jnp.maximum(room, 0))
    moved = jax.random.randint(jax.random.fold_in(own, 4), (amount // 2,), 0, 1 << 20) % (room + 1)
    lengths = lengths.at[source_of].add(-moved).at[receiver].add(moved)
    labels = jnp.searchsorted(jnp.cumsum(lengths), jnp.arange(rows * top), side="right").astype(jnp.int32)
    table = labels.reshape(top, rows).T
    table = table[jax.random.permutation(jax.random.fold_in(own, 1), rows)]
    rotation = jax.random.randint(jax.random.fold_in(own, 2), (rows, 1), 0, top)
    return jnp.take_along_axis(table, (jnp.arange(top)[None, :] + rotation) % top, axis=1)


def shares(count, total, reach, lean, full):
    portions = [(1 << 20) // math.isqrt(standing ** lean) + 1 for standing in range(1, count + 1)]
    largest = reach if full else min(reach, max(-(-total // count), total * portions[0] // sum(portions)))
    least = 1 if total - largest >= count - 1 else 0
    given, surplus = [largest] + [least] * (count - 1), total - largest - least * (count - 1)
    while surplus > 0:
        movable = [i for i in range(1, count) if given[i] < largest] or [i for i in range(1, count) if given[i] < reach]
        pool, remaining = sum([portions[i] for i in movable]), surplus
        for i in movable:
            more = min(reach - given[i], max(1, remaining * portions[i] // pool), surplus)
            given[i] = given[i] + more
            surplus = surplus - more
    return np.array(given)


def gaussian(rng, extent, spread, bound, cuts=(), held_as=jnp.bfloat16):
    values = spread * jax.random.normal(rng, extent, jnp.float32)
    if cuts:
        values = values * shard_levels(rng, extent, cuts, -0.22, 0.18)
    return jnp.clip(values, -bound, bound).astype(held_as)


def heavy_noise(own_key, extent, spread, limit, shards, heavy, kind=jnp.bfloat16):
    values = spread * jax.random.normal(own_key, extent, jnp.float32)
    if shards:
        values = values * shard_levels(own_key, extent, shards, -0.22, 0.18)
    return jnp.clip(with_spikes(values, jax.random.fold_in(own_key, 3), *heavy), -limit, limit).astype(kind)


def setup_inputs(seed: int = 0) -> dict:
    splits = jax.random.split(jax.random.key(seed), 14)
    inputs = draw_inputs(jax.random.fold_in(splits[13], 71), 0)
    attn_gain = jnp.clip(1.0 + 0.1 * jax.random.normal(splits[1], (MODEL_DIM,), jnp.float32), 0.5, 1.5).astype(jnp.bfloat16)
    query_weight = gaussian(splits[2], (MODEL_DIM, QUERY_HEADS * HEAD_DIM), MODEL_DIM ** -0.5, 0.1875, ((0, 16), (1, 2)))
    key_weight = gaussian(splits[3], (MODEL_DIM, KEY_VALUE_HEADS * HEAD_DIM), MODEL_DIM ** -0.5, 0.1875, ((0, 16), (1, 2)))
    value_matrix = gaussian(splits[4], (MODEL_DIM, KEY_VALUE_HEADS * HEAD_DIM), MODEL_DIM ** -0.5, 0.1875, ((0, 16), (1, 2)))
    output_weight = gaussian(splits[5], (MODEL_DIM, QUERY_HEADS * HEAD_DIM), 2 ** -0.5, 4.0, ((0, 16), (1, 2)))
    ffn_gain = jnp.clip(1.0 + 0.1 * jax.random.normal(splits[6], (MODEL_DIM,), jnp.float32), 0.5, 1.5).astype(jnp.bfloat16)
    gate_weight = gaussian(splits[7], (MODEL_DIM, EXPERT_COUNT, EXPERT_HIDDEN), MODEL_DIM ** -0.5, 0.1875, ((0, 16), (2, 2)))
    up_weight = gaussian(splits[8], (MODEL_DIM, EXPERT_COUNT, EXPERT_HIDDEN), MODEL_DIM ** -0.5, 0.1875, ((0, 16), (2, 2)))
    down_weight = gaussian(splits[9], (MODEL_DIM, EXPERT_COUNT, EXPERT_HIDDEN), 8 ** -0.5, 2.0, ((0, 16), (2, 2)))
    routes_keys = jax.random.split(jax.random.fold_in(splits[10], 1), SEQS * SEQUENCE_LENGTH // TOK_DEV)
    routes_turns = jax.random.permutation(jax.random.fold_in(splits[10], 3), SEQS * SEQUENCE_LENGTH // TOK_DEV)
    routes = jax.vmap(lambda own, number: routed_block(jax.random.fold_in(splits[10], 2), own, number, TOK_DEV, EXPERT_COUNT, TOP, CAP, 1))(routes_keys, routes_turns).reshape((SEQS, SEQUENCE_LENGTH, TOP))
    route_weights = jnp.clip(0.05 + 0.2 * jax.random.uniform(splits[11], (SEQS, SEQUENCE_LENGTH, TOP), jnp.float32) ** shard_levels(splits[11], (SEQS, SEQUENCE_LENGTH, TOP), ((0, 4), (1, 4)), -0.2, 0.2), 0.05, 0.25)
    cotangent = heavy_noise(splits[12], (SEQS, SEQUENCE_LENGTH, MODEL_DIM), 1.0, 6.0, ((0, 4), (1, 4)), (0, 2, 4, 2.0), jnp.float32)
    return dict(inputs=inputs, attn_gain=attn_gain, query_weight=query_weight, key_weight=key_weight, value_matrix=value_matrix, output_weight=output_weight, ffn_gain=ffn_gain, gate_weight=gate_weight, up_weight=up_weight, down_weight=down_weight, routes=routes, route_weights=route_weights, cotangent=cotangent)


EPS = 1e-06
SCORE_SCALE = 0.015625
RESIDUAL_SCALE = 0.22
ROPE_BASE = 10000.0
NEG = -1e+30

def rope_tables(positions, head_width):
    half_width = head_width // 2
    frequency = ROPE_BASE ** (-2.0 * jnp.arange(half_width, dtype=jnp.float32) / head_width)
    angles = positions.astype(jnp.float32)[:, None] * frequency[None, :]
    angles = jnp.concatenate([angles, angles], axis=1)
    return (jnp.cos(angles), jnp.sin(angles))

def apply_rotary(value_rows, cosine_table, rotary_sine_values):
    half_width = value_rows.shape[-1] // 2
    first_half = value_rows[..., :half_width]
    second_half = value_rows[..., half_width:]
    turned = jnp.concatenate([-second_half, first_half], axis=-1)
    return value_rows * cosine_table[:, None, :] + turned * rotary_sine_values[:, None, :]

def reverse_rotary(grads_in, cosine_table, rotary_sine_values):
    half_width = grads_in.shape[-1] // 2
    product = grads_in * rotary_sine_values[:, None, :]
    turned = jnp.concatenate([product[..., half_width:], -product[..., :half_width]], axis=-1)
    return grads_in * cosine_table[:, None, :] + turned

def inverse_rms(value_rows):
    return lax.rsqrt(lax.optimization_barrier(jnp.mean(value_rows * value_rows, axis=-1, keepdims=True)) + EPS)

def norm_backward(grad_normed, source, factor, gain_vector):
    scaled = grad_normed * gain_vector
    return factor * scaled - source * (factor * factor * factor) * lax.optimization_barrier(jnp.mean(scaled * source, axis=-1, keepdims=True))

def to_float_copy(value_rows):
    return value_rows.astype(jnp.float32)

def reference(inputs, attn_gain, query_weight, key_weight, value_matrix, output_weight, ffn_gain, gate_weight, up_weight, down_weight, routes, route_weights, cotangent):
    query_group_count = QUERY_HEADS // KEY_VALUE_HEADS
    blocks = N_CONTEXT
    gain_attn = to_float_copy(attn_gain)
    gain_ffn = to_float_copy(ffn_gain)
    gate_float = to_float_copy(gate_weight)
    up_float = to_float_copy(up_weight)
    down_float = to_float_copy(down_weight)
    cosine_table, rotary_sine_values = rope_tables(jnp.arange(SEQUENCE_LENGTH, dtype=jnp.int32), HEAD_DIM)
    block_starts = jnp.arange(blocks, dtype=jnp.int32) * TOK_DEV
    expert_ids = jnp.arange(EXPERT_COUNT, dtype=jnp.int32)
    key_positions = jnp.arange(SEQUENCE_LENGTH, dtype=jnp.int32)

    def one_sequence(carry, slices):
        tokens, routes_seq, weights_seq, grad_out = slices
        scale_one = inverse_rms(tokens)
        normed_one = (tokens * scale_one * gain_attn).astype(jnp.bfloat16)
        query_lin = jnp.dot(normed_one, query_weight, preferred_element_type=jnp.float32)
        linear_keys = jnp.dot(normed_one, key_weight, preferred_element_type=jnp.float32)
        value_rows = jnp.dot(normed_one, value_matrix, preferred_element_type=jnp.float32).astype(jnp.bfloat16)
        query_rows = apply_rotary(query_lin.reshape(SEQUENCE_LENGTH, QUERY_HEADS, HEAD_DIM), cosine_table, rotary_sine_values).astype(jnp.bfloat16)
        key_rows = apply_rotary(linear_keys.reshape(SEQUENCE_LENGTH, KEY_VALUE_HEADS, HEAD_DIM), cosine_table, rotary_sine_values).astype(jnp.bfloat16)
        query_wide_float = to_float_copy(query_rows).reshape(SEQUENCE_LENGTH, KEY_VALUE_HEADS, query_group_count, HEAD_DIM)
        key_float = to_float_copy(key_rows)
        value_wide_float = to_float_copy(value_rows).reshape(SEQUENCE_LENGTH, KEY_VALUE_HEADS, HEAD_DIM)

        def block_scores(start):
            query_block = lax.dynamic_slice_in_dim(query_wide_float, start, TOK_DEV, 0)
            scores = jnp.einsum('tkgd,skd->kgts', query_block, key_float) * SCORE_SCALE
            query_pos = start + jnp.arange(TOK_DEV, dtype=jnp.int32)
            visible = key_positions[None, :] <= query_pos[:, None]
            return (query_block, scores, visible)

        def attend(start):
            query_block, scores, visible = block_scores(start)
            masked = jnp.where(visible, scores, NEG)
            top_score = lax.optimization_barrier(jnp.max(masked, axis=-1, keepdims=True))
            row_total = lax.optimization_barrier(jnp.sum(jnp.where(visible, jnp.exp(scores - top_score), 0.0), axis=-1, keepdims=True))
            log_total = top_score + jnp.log(row_total)
            soft_b = jnp.where(visible, jnp.exp(scores - log_total), 0.0).astype(jnp.bfloat16)
            block_context = jnp.einsum('kgts,skd->tkgd', to_float_copy(soft_b), value_wide_float).astype(jnp.bfloat16)
            return (block_context, log_total[..., 0])
        contexts, log_totals = lax.map(attend, block_starts)
        attended_context = contexts.reshape(SEQUENCE_LENGTH, QUERY_HEADS * HEAD_DIM)
        attn_out = jnp.dot(attended_context, output_weight.T, preferred_element_type=jnp.float32)
        hidden = tokens + RESIDUAL_SCALE * attn_out
        scale_two = inverse_rms(hidden)
        normed_two = (hidden * scale_two * gain_ffn).astype(jnp.bfloat16)
        flat_routes = routes_seq.reshape(blocks, TOK_DEV * TOP).astype(jnp.int32)
        onehot = (flat_routes[..., None] == expert_ids).astype(jnp.int32)
        earlier = (jnp.cumsum(onehot, axis=1).astype(jnp.int32) - onehot) * onehot
        slots = lax.optimization_barrier(jnp.sum(earlier, axis=-1)).astype(jnp.int32)
        block_ids = jnp.arange(blocks, dtype=jnp.int32)[:, None]
        index_flat = ((block_ids * EXPERT_COUNT + flat_routes) * CAP + slots).reshape(-1).astype(jnp.int32)
        dispatched = jnp.zeros((blocks * EXPERT_COUNT * CAP, MODEL_DIM), jnp.bfloat16).at[index_flat].set(jnp.repeat(normed_two, TOP, axis=0)).reshape(blocks, EXPERT_COUNT, CAP, MODEL_DIM)
        disp_float = to_float_copy(dispatched)
        gate_act = jnp.einsum('becd,def->becf', disp_float, gate_float)
        up_act = jnp.einsum('becd,def->becf', disp_float, up_float)
        sigma = jax.nn.sigmoid(gate_act)
        swish = gate_act * sigma
        activated = (swish * up_act).astype(jnp.bfloat16)
        act_float = to_float_copy(activated)
        expert_out = jnp.einsum('becf,def->becd', act_float, down_float).reshape(-1, MODEL_DIM)
        picked = expert_out[index_flat].reshape(SEQUENCE_LENGTH, TOP, MODEL_DIM)
        moe = lax.optimization_barrier(jnp.sum(picked * weights_seq[..., None], axis=1))
        output = hidden + RESIDUAL_SCALE * moe
        grad_moe = RESIDUAL_SCALE * grad_out
        spread_rows = (weights_seq[..., None] * grad_moe[:, None, :]).reshape(SEQUENCE_LENGTH * TOP, MODEL_DIM).astype(jnp.bfloat16)
        grad_buffer = jnp.zeros((blocks * EXPERT_COUNT * CAP, MODEL_DIM), jnp.bfloat16).at[index_flat].set(spread_rows).reshape(blocks, EXPERT_COUNT, CAP, MODEL_DIM)
        buffer_float = to_float_copy(grad_buffer)
        grad_act = jnp.einsum('becd,def->becf', buffer_float, down_float)
        grad_swish = sigma * (1.0 + gate_act * (1.0 - sigma))
        grad_gate = (grad_act * up_act * grad_swish).astype(jnp.bfloat16)
        grad_up = (grad_act * swish).astype(jnp.bfloat16)
        gate_grad_float = to_float_copy(grad_gate)
        up_grad_float = to_float_copy(grad_up)
        sum_down = jnp.einsum('becd,becf->def', buffer_float, act_float)
        sum_gate = jnp.einsum('becd,becf->def', disp_float, gate_grad_float)
        sum_up = jnp.einsum('becd,becf->def', disp_float, up_grad_float)
        grad_disp = jnp.einsum('becf,def->becd', gate_grad_float, gate_float) + jnp.einsum('becf,def->becd', up_grad_float, up_float)
        grad_normed_two = lax.optimization_barrier(jnp.sum(grad_disp.reshape(-1, MODEL_DIM)[index_flat].reshape(SEQUENCE_LENGTH, TOP, MODEL_DIM), axis=1))
        sum_ffn_gain = lax.optimization_barrier(jnp.sum(grad_normed_two * hidden * scale_two, axis=0))
        grad_hidden = grad_out + norm_backward(grad_normed_two, hidden, scale_two, gain_ffn)
        grad_attn = (RESIDUAL_SCALE * grad_hidden).astype(jnp.bfloat16)
        sum_output = jnp.dot(grad_attn.T, attended_context, preferred_element_type=jnp.float32)
        context_gradient = jnp.dot(grad_attn, output_weight, preferred_element_type=jnp.float32).astype(jnp.bfloat16)
        context_gradient_wide = to_float_copy(context_gradient).reshape(SEQUENCE_LENGTH, KEY_VALUE_HEADS, query_group_count, HEAD_DIM)
        softmax_delta = lax.optimization_barrier(jnp.sum(context_gradient_wide * to_float_copy(attended_context).reshape(SEQUENCE_LENGTH, KEY_VALUE_HEADS, query_group_count, HEAD_DIM), axis=-1))

        def attend_back(kv_carry, block_input):
            key_gradient_rows, value_gradient_rows = kv_carry
            start, log_total = block_input
            query_block, scores, visible = block_scores(start)
            soft = jnp.where(visible, jnp.exp(scores - log_total[..., None]), 0.0)
            grad_block = lax.dynamic_slice_in_dim(context_gradient_wide, start, TOK_DEV, 0)
            delta_block = jnp.transpose(lax.dynamic_slice_in_dim(softmax_delta, start, TOK_DEV, 0), (1, 2, 0))
            value_gradient_rows = value_gradient_rows + jnp.einsum('kgts,tkgd->skd', to_float_copy(soft.astype(jnp.bfloat16)), grad_block)
            grad_soft = jnp.einsum('tkgd,skd->kgts', grad_block, value_wide_float)
            grad_scores = to_float_copy((soft * (grad_soft - delta_block[..., None])).astype(jnp.bfloat16))
            grad_query = SCORE_SCALE * jnp.einsum('kgts,skd->tkgd', grad_scores, key_float)
            key_gradient_rows = key_gradient_rows + SCORE_SCALE * jnp.einsum('kgts,tkgd->skd', grad_scores, query_block)
            return ((key_gradient_rows, value_gradient_rows), grad_query)
        empty_key_value = jnp.zeros((SEQUENCE_LENGTH, KEY_VALUE_HEADS, HEAD_DIM), jnp.float32)
        (key_gradient_rows, value_gradient_rows), grad_queries = lax.scan(attend_back, (empty_key_value, empty_key_value), (block_starts, log_totals))
        grad_query_lin = reverse_rotary(grad_queries.reshape(SEQUENCE_LENGTH, QUERY_HEADS, HEAD_DIM), cosine_table, rotary_sine_values).reshape(SEQUENCE_LENGTH, QUERY_HEADS * HEAD_DIM).astype(jnp.bfloat16)
        linear_key_gradient = reverse_rotary(key_gradient_rows, cosine_table, rotary_sine_values).reshape(SEQUENCE_LENGTH, KEY_VALUE_HEADS * HEAD_DIM).astype(jnp.bfloat16)
        value_gradient_second = value_gradient_rows.reshape(SEQUENCE_LENGTH, KEY_VALUE_HEADS * HEAD_DIM).astype(jnp.bfloat16)
        sum_query = jnp.dot(normed_one.T, grad_query_lin, preferred_element_type=jnp.float32)
        sum_key = jnp.dot(normed_one.T, linear_key_gradient, preferred_element_type=jnp.float32)
        sum_value = jnp.dot(normed_one.T, value_gradient_second, preferred_element_type=jnp.float32)
        grad_normed_one = jnp.dot(grad_query_lin, query_weight.T, preferred_element_type=jnp.float32) + jnp.dot(linear_key_gradient, key_weight.T, preferred_element_type=jnp.float32) + jnp.dot(value_gradient_second, value_matrix.T, preferred_element_type=jnp.float32)
        sum_attn_gain = lax.optimization_barrier(jnp.sum(grad_normed_one * tokens * scale_one, axis=0))
        grad_input = grad_hidden + norm_backward(grad_normed_one, tokens, scale_one, gain_attn)
        terms = (sum_attn_gain, sum_query, sum_key, sum_value, sum_output, sum_ffn_gain, sum_gate, sum_up, sum_down)
        new_carry = tuple((old + new for old, new in zip(carry, terms)))
        return (new_carry, (output, grad_input))
    initial_carry_state = (jnp.zeros((MODEL_DIM,), jnp.float32), jnp.zeros((MODEL_DIM, QUERY_HEADS * HEAD_DIM), jnp.float32), jnp.zeros((MODEL_DIM, KEY_VALUE_HEADS * HEAD_DIM), jnp.float32), jnp.zeros((MODEL_DIM, KEY_VALUE_HEADS * HEAD_DIM), jnp.float32), jnp.zeros((MODEL_DIM, QUERY_HEADS * HEAD_DIM), jnp.float32), jnp.zeros((MODEL_DIM,), jnp.float32), jnp.zeros((MODEL_DIM, EXPERT_COUNT, EXPERT_HIDDEN), jnp.float32), jnp.zeros((MODEL_DIM, EXPERT_COUNT, EXPERT_HIDDEN), jnp.float32), jnp.zeros((MODEL_DIM, EXPERT_COUNT, EXPERT_HIDDEN), jnp.float32))
    sums, (output, grad_input) = lax.scan(one_sequence, initial_carry_state, (inputs, routes, route_weights, cotangent))
    return (output, grad_input, sums[0], sums[1], sums[2], sums[3], sums[4], sums[5], sums[6], sums[7], sums[8])
```

```python
import jax
import jax.numpy as jnp
from jax import lax
from jax.sharding import PartitionSpec as P

HEAD_DIM = 64


EPS = 1e-06
SCORE_SCALE = 0.015625
RESIDUAL_SCALE = 0.22
ROPE_BASE = 10000.0
NEG = -1e30


def rope_tables(positions, head_width):
    half_width = head_width // 2
    frequency = ROPE_BASE ** (-2.0 * jnp.arange(half_width, dtype=jnp.float32) / head_width)
    angles = positions.astype(jnp.float32)[:, None] * frequency[None, :]
    angles = jnp.concatenate([angles, angles], axis=1)
    return (jnp.cos(angles), jnp.sin(angles))


def apply_rotary(value_rows, cosine_table, rotary_sine_values):
    half_width = value_rows.shape[-1] // 2
    first_half = value_rows[..., :half_width]
    second_half = value_rows[..., half_width:]
    turned = jnp.concatenate([-second_half, first_half], axis=-1)
    return value_rows * cosine_table[:, None, :] + turned * rotary_sine_values[:, None, :]


def reverse_rotary(grads_in, cosine_table, rotary_sine_values):
    half_width = grads_in.shape[-1] // 2
    product = grads_in * rotary_sine_values[:, None, :]
    turned = jnp.concatenate([product[..., half_width:], -product[..., :half_width]], axis=-1)
    return grads_in * cosine_table[:, None, :] + turned


def inverse_rms(value_rows):
    return lax.rsqrt(jnp.mean(value_rows * value_rows, axis=-1, keepdims=True) + EPS)


def norm_backward(grad_normed, source, factor, gain_vector):
    scaled = grad_normed * gain_vector
    return factor * scaled - source * (factor * factor * factor) * jnp.mean(
        scaled * source, axis=-1, keepdims=True
    )


def contract_rows(left, right):
    return lax.dot_general(
        left, right, (((0,), (0,)), ((), ())), preferred_element_type=jnp.float32
    )


def contract_cols(left, right):
    return lax.dot_general(
        left, right, (((1,), (1,)), ((), ())), preferred_element_type=jnp.float32
    )


def exchange(array, axis, bit):
    size = lax.axis_size(axis)
    return lax.ppermute(array, axis, [(i, i ^ bit) for i in range(size)])


def pair_sum(part, axis):
    kept = lax.reduce_precision(part, 8, 7)
    return kept + exchange(kept.astype(jnp.bfloat16), axis, 1).astype(jnp.float32)


def axis_bits(axis):
    size = lax.axis_size(axis)
    bits = []
    bit = 1
    while bit < size:
        bits.append(bit)
        bit *= 2
    return bits


def halving_sum(terms, axis, dim):
    index = lax.axis_index(axis)
    for bit in axis_bits(axis):
        shape = terms.shape
        pairs = terms.reshape(shape[:dim] + (shape[dim] // 2, 2) + shape[dim + 1 :])
        mine = (index // bit) % 2
        low = lax.index_in_dim(pairs, 0, dim + 1, keepdims=False)
        high = lax.index_in_dim(pairs, 1, dim + 1, keepdims=False)
        sent = jnp.where(mine == 0, high, low).astype(jnp.bfloat16)
        kept = jnp.where(mine == 0, low, high)
        terms = kept.astype(jnp.float32) + exchange(sent, axis, bit).astype(jnp.float32)
    return lax.index_in_dim(terms, 0, dim, keepdims=False)


def relative_gather(block, axis):
    blocks = block[None]
    for bit in axis_bits(axis):
        blocks = jnp.concatenate([blocks, exchange(blocks, axis, bit)], axis=0)
    return blocks


def relative_sum(blocks, axis):
    for bit in reversed(axis_bits(axis)):
        received = exchange(blocks[bit:].astype(jnp.bfloat16), axis, bit)
        blocks = blocks[:bit] + received.astype(jnp.float32)
    return blocks[0]


def body(
    inputs,
    attn_gain,
    query_weight,
    key_weight,
    value_matrix,
    output_weight,
    ffn_gain,
    gate_weight,
    up_weight,
    down_weight,
    routes,
    route_weights,
    cotangent,
):
    f32, b16 = jnp.float32, jnp.bfloat16
    shard_count = lax.axis_size("shard")
    context_count = lax.axis_size("context")
    tokens = inputs[0]
    length, model_width = tokens.shape
    rows_own = query_weight.shape[0]
    q_cols, kv_cols = query_weight.shape[1], key_weight.shape[1]
    qkv_cols = q_cols + 2 * kv_cols
    kv_heads = kv_cols // HEAD_DIM
    heads = q_cols // HEAD_DIM
    group = heads // kv_heads
    experts, hidden_units = gate_weight.shape[1], gate_weight.shape[2]
    own_experts = experts // shard_count
    own_cols = own_experts * hidden_units

    gains = jnp.pad(jnp.stack([attn_gain, ffn_gain], axis=1), ((0, 0), (0, 126)))
    packed = jnp.concatenate(
        [query_weight, key_weight, value_matrix, output_weight, gains], axis=1
    )
    full = lax.all_gather(packed, ("shard", "context"), axis=0, tiled=True)
    qkv_full = full[:, :qkv_cols]
    output_full = full[:, qkv_cols : qkv_cols + q_cols]
    gain_rows = full[:, qkv_cols + q_cols :].astype(f32).T
    gain_attn, gain_ffn = gain_rows[0], gain_rows[1]

    grad_out = cotangent[0]
    expert_ids = jnp.arange(experts, dtype=jnp.int32)
    dense = jnp.sum(
        jnp.where(routes[0][:, :, None] == expert_ids, route_weights[0][:, :, None], 0.0), axis=1
    )
    dense_high = lax.reduce_precision(dense, 8, 7)
    dense_low = dense - dense_high
    early = jnp.concatenate(
        [
            grad_out.astype(b16),
            dense_high.astype(b16),
            dense_low.astype(b16),
            jnp.zeros((length, 128 - 2 * experts), b16),
        ],
        axis=1,
    )
    early_all = lax.all_gather(early, "shard", axis=0, tiled=True)

    stacked_weights = jnp.stack([gate_weight, up_weight, down_weight], axis=0)
    stacked_weights = stacked_weights.reshape(3, rows_own, shard_count, own_cols)
    stacked_weights = jnp.transpose(stacked_weights, (2, 0, 1, 3))
    owner = lax.all_to_all(stacked_weights, "shard", split_axis=0, concat_axis=0, tiled=True)
    expert_weights = lax.all_gather(owner, "context", axis=0, tiled=False)
    expert_weights = jnp.transpose(expert_weights, (2, 1, 0, 3, 4)).reshape(
        3, model_width, own_cols
    )
    own_gate, own_up, own_down = expert_weights[0], expert_weights[1], expert_weights[2]

    context_index = lax.axis_index("context")
    positions = context_index * length + jnp.arange(length, dtype=jnp.int32)
    cosine_table, rotary_sine_values = rope_tables(positions, HEAD_DIM)
    scale_one = inverse_rms(tokens)
    normed_one = (tokens * scale_one * gain_attn).astype(b16)
    qkv_lin = jnp.dot(normed_one, qkv_full, preferred_element_type=f32)
    turned = apply_rotary(
        qkv_lin[:, : q_cols + kv_cols].reshape(length, heads + kv_heads, HEAD_DIM),
        cosine_table,
        rotary_sine_values,
    ).astype(b16)
    query_rows = turned[:, :heads].reshape(length, kv_heads, group, HEAD_DIM)
    key_rows = turned[:, heads:].reshape(length, kv_cols)
    kv_rows = jnp.concatenate([key_rows, qkv_lin[:, q_cols + kv_cols :].astype(b16)], axis=1)
    kv_all = relative_gather(kv_rows, "context").reshape(context_count * length, 2 * kv_cols)
    keys = kv_all[:, :kv_cols].reshape(-1, kv_heads, HEAD_DIM)
    values = kv_all[:, kv_cols:].reshape(-1, kv_heads, HEAD_DIM)
    owners = context_index ^ jnp.arange(context_count, dtype=jnp.int32)
    key_pos = (
        owners[:, None] * length + jnp.arange(length, dtype=jnp.int32)[None, :]
    ).reshape(-1)
    visible = key_pos[None, :] <= positions[:, None]
    scores = (
        jnp.einsum("tkgd,skd->kgts", query_rows, keys, preferred_element_type=f32) * SCORE_SCALE
    )
    masked = jnp.where(visible, scores, NEG)
    weights_exp = jnp.where(visible, jnp.exp(masked - jnp.max(masked, -1, keepdims=True)), 0.0)
    soft = weights_exp / jnp.sum(weights_exp, axis=-1, keepdims=True)
    soft_b = soft.astype(b16)
    attended = jnp.einsum("kgts,skd->tkgd", soft_b, values, preferred_element_type=f32).astype(b16)
    attended_context = attended.reshape(length, q_cols)
    attn_out = pair_sum(contract_cols(attended_context, output_full), "tensor")
    hidden = tokens + RESIDUAL_SCALE * attn_out
    scale_two = inverse_rms(hidden)
    normed_two = (hidden * scale_two * gain_ffn).astype(b16)

    x_all = lax.all_gather(normed_two, "shard", axis=0, tiled=True)
    g_all = early_all[:, :model_width]
    dense_all = early_all[:, model_width : model_width + experts].astype(f32) + early_all[
        :, model_width + experts : model_width + 2 * experts
    ].astype(f32)
    dense_own = lax.dynamic_slice_in_dim(
        dense_all, lax.axis_index("shard") * own_experts, own_experts, 1
    )
    spread = jnp.repeat(dense_own, hidden_units, axis=1)
    grad_act = contract_dense(g_all, own_down) * (RESIDUAL_SCALE * spread)
    gate_act = contract_dense(x_all, own_gate)
    up_act = contract_dense(x_all, own_up)
    sigma = jax.nn.sigmoid(gate_act)
    swish = gate_act * sigma
    activated = (swish * up_act * spread).astype(b16)
    grad_gate = (grad_act * up_act * sigma * (1.0 + gate_act * (1.0 - sigma))).astype(b16)
    grad_up = (grad_act * swish).astype(b16)
    normed_two_terms = (contract_cols(grad_gate, own_gate) + contract_cols(grad_up, own_up)).astype(
        b16
    )
    normed_two_parts = lax.all_to_all(
        normed_two_terms.reshape(shard_count, length, model_width), "shard", 0, 0, tiled=True
    )
    moe_terms = contract_cols(activated, own_down).astype(b16)
    moe_parts = lax.all_to_all(
        moe_terms.reshape(shard_count, length, model_width), "shard", 0, 0, tiled=True
    )
    grad_normed_two = pair_sum(jnp.sum(normed_two_parts.astype(f32), axis=0), "tensor")
    moe = pair_sum(jnp.sum(moe_parts.astype(f32), axis=0), "tensor")
    output = hidden + RESIDUAL_SCALE * moe

    expert_terms = jnp.stack(
        [
            contract_rows(x_all, grad_gate),
            contract_rows(x_all, grad_up),
            RESIDUAL_SCALE * contract_rows(g_all, activated),
        ],
        axis=0,
    ).astype(b16)
    expert_terms = jnp.transpose(
        expert_terms.reshape(3, shard_count, context_count, rows_own, own_cols), (1, 2, 0, 3, 4)
    )
    context_sums = halving_sum(expert_terms, "context", 1).astype(b16)
    expert_sums = lax.all_to_all(context_sums, "shard", 0, 0, tiled=True)
    expert_sums = (
        jnp.transpose(expert_sums, (1, 2, 0, 3))
        .reshape(3, rows_own, experts, hidden_units)
        .astype(f32)
    )

    term_ffn_gain = jnp.sum(grad_normed_two * hidden * scale_two, axis=0)
    grad_hidden = grad_out + norm_backward(grad_normed_two, hidden, scale_two, gain_ffn)
    grad_attn = (RESIDUAL_SCALE * grad_hidden).astype(b16)
    context_gradient = jnp.dot(grad_attn, output_full, preferred_element_type=f32).astype(b16)
    grad_heads = context_gradient.reshape(length, kv_heads, group, HEAD_DIM)
    delta = jnp.transpose(
        jnp.sum(grad_heads.astype(f32) * attended.astype(f32), axis=-1), (1, 2, 0)
    )
    grad_soft = jnp.einsum("tkgd,skd->kgts", grad_heads, values, preferred_element_type=f32)
    grad_scores = (soft * (grad_soft - delta[..., None])).astype(b16)
    value_term = jnp.einsum("kgts,tkgd->skd", soft_b, grad_heads, preferred_element_type=f32)
    key_term = SCORE_SCALE * jnp.einsum(
        "kgts,tkgd->skd", grad_scores, query_rows, preferred_element_type=f32
    )
    kv_terms = jnp.concatenate(
        [key_term.reshape(-1, kv_cols), value_term.reshape(-1, kv_cols)], axis=1
    ).reshape(context_count, length, 2 * kv_cols)
    kv_sum = relative_sum(kv_terms, "context")
    grad_query = SCORE_SCALE * jnp.einsum(
        "kgts,skd->tkgd", grad_scores, keys, preferred_element_type=f32
    )
    term_output = contract_rows(grad_attn, attended_context)
    turned_back = reverse_rotary(
        jnp.concatenate(
            [
                grad_query.reshape(length, heads, HEAD_DIM),
                kv_sum[:, :kv_cols].reshape(length, kv_heads, HEAD_DIM),
            ],
            axis=1,
        ),
        cosine_table,
        rotary_sine_values,
    ).reshape(length, q_cols + kv_cols)
    grad_qkv = jnp.concatenate([turned_back, kv_sum[:, kv_cols:]], axis=1).astype(b16)
    term_qkv = contract_rows(normed_one, grad_qkv)
    normed_one_part = contract_cols(grad_qkv, qkv_full)
    term_attn_gain = jnp.sum(normed_one_part * tokens * scale_one, axis=0)
    gain_terms = jnp.pad(jnp.stack([term_attn_gain, term_ffn_gain], axis=0), ((0, 126), (0, 0))).T
    sum_output = scatter_rows(term_output, shard_count, context_count)
    sum_rest = scatter_rows(
        jnp.concatenate([term_qkv, gain_terms], axis=1), shard_count, context_count
    )
    grad_normed_one = pair_sum(normed_one_part, "tensor")
    grad_input = grad_hidden + norm_backward(grad_normed_one, tokens, scale_one, gain_attn)
    own_gains = sum_rest[:, qkv_cols:]
    sum_attn_gain = (own_gains + exchange(own_gains, "tensor", 1))[:, 0]
    return (
        output[None],
        grad_input[None],
        sum_attn_gain,
        sum_rest[:, :q_cols],
        sum_rest[:, q_cols : q_cols + kv_cols],
        sum_rest[:, q_cols + kv_cols : qkv_cols],
        sum_output,
        own_gains[:, 1],
        expert_sums[0],
        expert_sums[1],
        expert_sums[2],
    )


def contract_dense(left, right):
    return jnp.dot(left, right, preferred_element_type=jnp.float32)


def scatter_rows(term, shard_count, context_count):
    split = term.reshape(shard_count, context_count, -1, term.shape[1])
    return halving_sum(halving_sum(split, "context", 1), "shard", 0)


def solution(mesh):
    placed = (
        P("shard", "context", None),
        P(("shard", "context")),
        P(("shard", "context"), "tensor"),
        P(("shard", "context"), "tensor"),
        P(("shard", "context"), "tensor"),
        P(("shard", "context"), "tensor"),
        P(("shard", "context")),
        P(("shard", "context"), None, "tensor"),
        P(("shard", "context"), None, "tensor"),
        P(("shard", "context"), None, "tensor"),
        P("shard", "context", None),
        P("shard", "context", None),
        P("shard", "context", None),
    )
    return jax.shard_map(
        body,
        mesh=mesh,
        in_specs=placed,
        out_specs=(
            P("shard", "context", None),
            P("shard", "context", None),
            P(("shard", "context")),
            P(("shard", "context"), "tensor"),
            P(("shard", "context"), "tensor"),
            P(("shard", "context"), "tensor"),
            P(("shard", "context"), "tensor"),
            P(("shard", "context")),
            P(("shard", "context"), None, "tensor"),
            P(("shard", "context"), None, "tensor"),
            P(("shard", "context"), None, "tensor"),
        ),
        check_vma=False,
    )
```

```python
import jax
import jax.numpy as jnp
from jax import lax
from jax.sharding import PartitionSpec as P

HEAD_DIM = 64


EPS = 1e-06
SCORE_SCALE = 0.015625
RESIDUAL_SCALE = 0.22
ROPE_BASE = 10000.0
NEG = -1e30


def rope_tables(positions, head_width):
    half_width = head_width // 2
    frequency = ROPE_BASE ** (-2.0 * jnp.arange(half_width, dtype=jnp.float32) / head_width)
    angles = positions.astype(jnp.float32)[:, None] * frequency[None, :]
    angles = jnp.concatenate([angles, angles], axis=1)
    return (jnp.cos(angles), jnp.sin(angles))


def apply_rotary(value_rows, cosine_table, rotary_sine_values):
    half_width = value_rows.shape[-1] // 2
    first_half = value_rows[..., :half_width]
    second_half = value_rows[..., half_width:]
    turned = jnp.concatenate([-second_half, first_half], axis=-1)
    return value_rows * cosine_table[:, None, :] + turned * rotary_sine_values[:, None, :]


def reverse_rotary(grads_in, cosine_table, rotary_sine_values):
    half_width = grads_in.shape[-1] // 2
    product = grads_in * rotary_sine_values[:, None, :]
    turned = jnp.concatenate([product[..., half_width:], -product[..., :half_width]], axis=-1)
    return grads_in * cosine_table[:, None, :] + turned


def inverse_rms(value_rows):
    return lax.rsqrt(jnp.mean(value_rows * value_rows, axis=-1, keepdims=True) + EPS)


def norm_backward(grad_normed, source, factor, gain_vector):
    scaled = grad_normed * gain_vector
    return factor * scaled - source * (factor * factor * factor) * jnp.mean(
        scaled * source, axis=-1, keepdims=True
    )


def contract_rows(left, right):
    return lax.dot_general(
        left, right, (((0,), (0,)), ((), ())), preferred_element_type=jnp.float32
    )


def contract_cols(left, right):
    return lax.dot_general(
        left, right, (((1,), (1,)), ((), ())), preferred_element_type=jnp.float32
    )


def exchange(array, axis, bit):
    size = lax.axis_size(axis)
    return lax.ppermute(array, axis, [(i, i ^ bit) for i in range(size)])


def pair_sum(part, axis):
    kept = lax.reduce_precision(part, 8, 7)
    return kept + exchange(kept.astype(jnp.bfloat16), axis, 1).astype(jnp.float32)


def axis_bits(axis):
    size = lax.axis_size(axis)
    bits = []
    bit = 1
    while bit < size:
        bits.append(bit)
        bit *= 2
    return bits


def tie(*arrays):
    return lax.optimization_barrier(arrays)


def halving_step(terms, axis, dim, bit):
    shape = terms.shape
    pairs = terms.reshape(shape[:dim] + (shape[dim] // 2, 2) + shape[dim + 1 :])
    mine = (lax.axis_index(axis) // bit) % 2
    low = lax.index_in_dim(pairs, 0, dim + 1, keepdims=False)
    high = lax.index_in_dim(pairs, 1, dim + 1, keepdims=False)
    sent = jnp.where(mine == 0, high, low).astype(jnp.bfloat16)
    kept = jnp.where(mine == 0, low, high)
    return kept.astype(jnp.float32) + exchange(sent, axis, bit).astype(jnp.float32)


def halving_sum(terms, axis, dim):
    for bit in axis_bits(axis):
        terms = halving_step(terms, axis, dim, bit)
    return lax.index_in_dim(terms, 0, dim, keepdims=False)


def ordered_step(blocks, axis, bit):
    received = exchange(blocks, axis, bit)
    mine = (lax.axis_index(axis) // bit) % 2
    low = jnp.where(mine == 0, blocks, received)
    high = jnp.where(mine == 0, received, blocks)
    return jnp.stack([low, high], axis=1).reshape((-1,) + blocks.shape[1:])


def relative_gather(block, axis):
    blocks = block[None]
    offsets = [0]
    for bit in reversed(axis_bits(axis)):
        blocks = jnp.concatenate([blocks, exchange(blocks, axis, bit)], axis=0)
        offsets = offsets + [offset ^ bit for offset in offsets]
    return blocks, offsets


def relative_sum(blocks, axis):
    for bit in axis_bits(axis):
        half = blocks.shape[0] // 2
        received = exchange(blocks[half:].astype(jnp.bfloat16), axis, bit)
        blocks = blocks[:half] + received.astype(jnp.float32)
    return blocks[0]


def body(
    inputs,
    attn_gain,
    query_weight,
    key_weight,
    value_matrix,
    output_weight,
    ffn_gain,
    gate_weight,
    up_weight,
    down_weight,
    routes,
    route_weights,
    cotangent,
):
    f32, b16 = jnp.float32, jnp.bfloat16
    shard_count = lax.axis_size("shard")
    context_count = lax.axis_size("context")
    tokens = inputs[0]
    length, model_width = tokens.shape
    rows_own = query_weight.shape[0]
    q_cols, kv_cols = query_weight.shape[1], key_weight.shape[1]
    qkv_cols = q_cols + 2 * kv_cols
    kv_heads = kv_cols // HEAD_DIM
    heads = q_cols // HEAD_DIM
    group = heads // kv_heads
    experts, hidden_units = gate_weight.shape[1], gate_weight.shape[2]
    own_experts = experts // shard_count
    own_cols = own_experts * hidden_units

    gains = jnp.pad(jnp.stack([attn_gain, ffn_gain], axis=1), ((0, 0), (0, 126)))
    packed = jnp.concatenate(
        [query_weight, key_weight, value_matrix, output_weight, gains], axis=1
    )
    packed_all = lax.all_gather(packed, "shard", axis=0, tiled=False)

    grad_out = cotangent[0]
    expert_ids = jnp.arange(experts, dtype=jnp.int32)
    dense = jnp.sum(
        jnp.where(routes[0][:, :, None] == expert_ids, route_weights[0][:, :, None], 0.0), axis=1
    )
    dense_high = lax.reduce_precision(dense, 8, 7)
    dense_low = dense - dense_high
    early = jnp.concatenate(
        [
            grad_out.astype(b16),
            dense_high.astype(b16),
            dense_low.astype(b16),
            jnp.zeros((length, 128 - 2 * experts), b16),
        ],
        axis=1,
    )
    packed_all, early = tie(packed_all, early)
    early_all = lax.all_gather(early, "shard", axis=0, tiled=True)

    bits = axis_bits("context")
    full = packed_all[None]
    for bit in reversed(bits):
        full = ordered_step(full, "context", bit)
    full = jnp.swapaxes(full, 0, 1).reshape(model_width, packed.shape[1])
    qkv_full = full[:, :qkv_cols]
    output_full = full[:, qkv_cols : qkv_cols + q_cols]
    gain_rows = full[:, qkv_cols + q_cols :].astype(f32).T
    gain_attn, gain_ffn = gain_rows[0], gain_rows[1]

    stacked_weights = jnp.stack([gate_weight, up_weight, down_weight], axis=0)
    stacked_weights = stacked_weights.reshape(3, rows_own, shard_count, own_cols)
    stacked_weights = jnp.transpose(stacked_weights, (2, 0, 1, 3))
    owner = lax.all_to_all(stacked_weights, "shard", split_axis=0, concat_axis=0, tiled=True)
    qkv_full, owner = tie(qkv_full, owner)
    expert_blocks = owner[None]
    for bit in reversed(bits[1:]):
        expert_blocks = ordered_step(expert_blocks, "context", bit)

    context_index = lax.axis_index("context")
    positions = context_index * length + jnp.arange(length, dtype=jnp.int32)
    cosine_table, rotary_sine_values = rope_tables(positions, HEAD_DIM)
    scale_one = inverse_rms(tokens)
    normed_one = (tokens * scale_one * gain_attn).astype(b16)
    qkv_lin = jnp.dot(normed_one, qkv_full, preferred_element_type=f32)
    turned = apply_rotary(
        qkv_lin[:, : q_cols + kv_cols].reshape(length, heads + kv_heads, HEAD_DIM),
        cosine_table,
        rotary_sine_values,
    ).astype(b16)
    query_rows = turned[:, :heads].reshape(length, kv_heads, group, HEAD_DIM)
    key_rows = turned[:, heads:].reshape(length, kv_cols)
    kv_rows = jnp.concatenate([key_rows, qkv_lin[:, q_cols + kv_cols :].astype(b16)], axis=1)
    kv_blocks, offsets = relative_gather(kv_rows, "context")
    kv_all = kv_blocks.reshape(context_count * length, 2 * kv_cols)
    keys = kv_all[:, :kv_cols].reshape(-1, kv_heads, HEAD_DIM)
    values = kv_all[:, kv_cols:].reshape(-1, kv_heads, HEAD_DIM)
    owners = context_index ^ jnp.array(offsets, dtype=jnp.int32)
    key_pos = (
        owners[:, None] * length + jnp.arange(length, dtype=jnp.int32)[None, :]
    ).reshape(-1)
    visible = key_pos[None, :] <= positions[:, None]
    scores = (
        jnp.einsum("tkgd,skd->kgts", query_rows, keys, preferred_element_type=f32) * SCORE_SCALE
    )
    masked = jnp.where(visible, scores, NEG)
    weights_exp = jnp.where(visible, jnp.exp(masked - jnp.max(masked, -1, keepdims=True)), 0.0)
    soft = weights_exp / jnp.sum(weights_exp, axis=-1, keepdims=True)
    soft_b = soft.astype(b16)
    attended = jnp.einsum("kgts,skd->tkgd", soft_b, values, preferred_element_type=f32).astype(b16)
    attended_context = attended.reshape(length, q_cols)
    attn_out = pair_sum(contract_cols(attended_context, output_full), "tensor")
    hidden = tokens + RESIDUAL_SCALE * attn_out
    scale_two = inverse_rms(hidden)
    normed_two = (hidden * scale_two * gain_ffn).astype(b16)

    normed_two, expert_blocks = tie(normed_two, expert_blocks)
    expert_blocks = ordered_step(expert_blocks, "context", 1)
    expert_weights = jnp.transpose(expert_blocks, (2, 1, 0, 3, 4)).reshape(
        3, model_width, own_cols
    )
    own_gate, own_up, own_down = expert_weights[0], expert_weights[1], expert_weights[2]
    x_all = lax.all_gather(normed_two, "shard", axis=0, tiled=True)
    g_all = early_all[:, :model_width]
    dense_all = early_all[:, model_width : model_width + experts].astype(f32) + early_all[
        :, model_width + experts : model_width + 2 * experts
    ].astype(f32)
    dense_own = lax.dynamic_slice_in_dim(
        dense_all, lax.axis_index("shard") * own_experts, own_experts, 1
    )
    spread = jnp.repeat(dense_own, hidden_units, axis=1)
    grad_act = contract_dense(g_all, own_down) * (RESIDUAL_SCALE * spread)
    gate_act = contract_dense(x_all, own_gate)
    up_act = contract_dense(x_all, own_up)
    sigma = jax.nn.sigmoid(gate_act)
    swish = gate_act * sigma
    activated = (swish * up_act * spread).astype(b16)
    grad_gate = (grad_act * up_act * sigma * (1.0 + gate_act * (1.0 - sigma))).astype(b16)
    grad_up = (grad_act * swish).astype(b16)
    normed_two_terms = (contract_cols(grad_gate, own_gate) + contract_cols(grad_up, own_up)).astype(
        b16
    )
    normed_two_parts = lax.all_to_all(
        normed_two_terms.reshape(shard_count, length, model_width), "shard", 0, 0, tiled=True
    )
    moe_terms = contract_cols(activated, own_down).astype(b16)
    moe_parts = lax.all_to_all(
        moe_terms.reshape(shard_count, length, model_width), "shard", 0, 0, tiled=True
    )
    grad_normed_two = pair_sum(jnp.sum(normed_two_parts.astype(f32), axis=0), "tensor")

    expert_terms = jnp.stack(
        [
            contract_rows(x_all, grad_gate),
            contract_rows(x_all, grad_up),
            RESIDUAL_SCALE * contract_rows(g_all, activated),
        ],
        axis=0,
    ).astype(b16)
    expert_terms = jnp.transpose(
        expert_terms.reshape(3, shard_count, context_count, rows_own, own_cols), (1, 2, 0, 3, 4)
    )
    expert_terms = halving_step(expert_terms, "context", 1, 1)

    term_ffn_gain = jnp.sum(grad_normed_two * hidden * scale_two, axis=0)
    grad_hidden = grad_out + norm_backward(grad_normed_two, hidden, scale_two, gain_ffn)
    grad_attn = (RESIDUAL_SCALE * grad_hidden).astype(b16)
    grad_attn, expert_terms = tie(grad_attn, expert_terms)
    for bit in bits[1:]:
        expert_terms = halving_step(expert_terms, "context", 1, bit)
    context_sums = expert_terms[:, 0].astype(b16)
    context_gradient = jnp.dot(grad_attn, output_full, preferred_element_type=f32).astype(b16)
    grad_heads = context_gradient.reshape(length, kv_heads, group, HEAD_DIM)
    delta = jnp.transpose(
        jnp.sum(grad_heads.astype(f32) * attended.astype(f32), axis=-1), (1, 2, 0)
    )
    grad_soft = jnp.einsum("tkgd,skd->kgts", grad_heads, values, preferred_element_type=f32)
    grad_scores = (soft * (grad_soft - delta[..., None])).astype(b16)
    value_term = jnp.einsum("kgts,tkgd->skd", soft_b, grad_heads, preferred_element_type=f32)
    key_term = SCORE_SCALE * jnp.einsum(
        "kgts,tkgd->skd", grad_scores, query_rows, preferred_element_type=f32
    )
    kv_terms = jnp.concatenate(
        [key_term.reshape(-1, kv_cols), value_term.reshape(-1, kv_cols)], axis=1
    ).reshape(context_count, length, 2 * kv_cols)
    kv_sum = relative_sum(kv_terms, "context")
    kv_sum, moe_parts, context_sums = tie(kv_sum, moe_parts, context_sums)
    moe = pair_sum(jnp.sum(moe_parts.astype(f32), axis=0), "tensor")
    output = hidden + RESIDUAL_SCALE * moe
    expert_sums = lax.all_to_all(context_sums, "shard", 0, 0, tiled=True)
    expert_sums = (
        jnp.transpose(expert_sums, (1, 2, 0, 3))
        .reshape(3, rows_own, experts, hidden_units)
        .astype(f32)
    )
    grad_query = SCORE_SCALE * jnp.einsum(
        "kgts,skd->tkgd", grad_scores, keys, preferred_element_type=f32
    )
    term_output = contract_rows(grad_attn, attended_context)
    turned_back = reverse_rotary(
        jnp.concatenate(
            [
                grad_query.reshape(length, heads, HEAD_DIM),
                kv_sum[:, :kv_cols].reshape(length, kv_heads, HEAD_DIM),
            ],
            axis=1,
        ),
        cosine_table,
        rotary_sine_values,
    ).reshape(length, q_cols + kv_cols)
    grad_qkv = jnp.concatenate([turned_back, kv_sum[:, kv_cols:]], axis=1).astype(b16)
    term_qkv = contract_rows(normed_one, grad_qkv)
    normed_one_part = contract_cols(grad_qkv, qkv_full)
    term_attn_gain = jnp.sum(normed_one_part * tokens * scale_one, axis=0)
    gain_terms = jnp.concatenate(
        [term_attn_gain.reshape(-1, rows_own), term_ffn_gain.reshape(-1, rows_own)], axis=1
    )
    sum_output = scatter_rows(term_output, shard_count, context_count)
    sum_rest = scatter_rows(term_qkv, shard_count, context_count)
    own_gains = scatter_rows(gain_terms, shard_count, context_count)
    grad_normed_one = pair_sum(normed_one_part, "tensor")
    grad_input = grad_hidden + norm_backward(grad_normed_one, tokens, scale_one, gain_attn)
    sum_attn_gain = (own_gains + exchange(own_gains, "tensor", 1))[0, :rows_own]
    return (
        output[None],
        grad_input[None],
        sum_attn_gain,
        sum_rest[:, :q_cols],
        sum_rest[:, q_cols : q_cols + kv_cols],
        sum_rest[:, q_cols + kv_cols : qkv_cols],
        sum_output,
        own_gains[0, rows_own:],
        expert_sums[0],
        expert_sums[1],
        expert_sums[2],
    )


def contract_dense(left, right):
    return jnp.dot(left, right, preferred_element_type=jnp.float32)


def scatter_rows(term, shard_count, context_count):
    split = term.reshape(shard_count, context_count, -1, term.shape[1])
    return halving_sum(halving_sum(split, "context", 1), "shard", 0)


def solution(mesh):
    placed = (
        P("shard", "context", None),
        P(("shard", "context")),
        P(("shard", "context"), "tensor"),
        P(("shard", "context"), "tensor"),
        P(("shard", "context"), "tensor"),
        P(("shard", "context"), "tensor"),
        P(("shard", "context")),
        P(("shard", "context"), None, "tensor"),
        P(("shard", "context"), None, "tensor"),
        P(("shard", "context"), None, "tensor"),
        P("shard", "context", None),
        P("shard", "context", None),
        P("shard", "context", None),
    )
    return jax.shard_map(
        body,
        mesh=mesh,
        in_specs=placed,
        out_specs=(
            P("shard", "context", None),
            P("shard", "context", None),
            P(("shard", "context")),
            P(("shard", "context"), "tensor"),
            P(("shard", "context"), "tensor"),
            P(("shard", "context"), "tensor"),
            P(("shard", "context"), "tensor"),
            P(("shard", "context")),
            P(("shard", "context"), None, "tensor"),
            P(("shard", "context"), None, "tensor"),
            P(("shard", "context"), None, "tensor"),
        ),
        check_vma=False,
    )
```

```python
import jax
import jax.numpy as jnp
from jax import lax
from jax.sharding import PartitionSpec as P

HEAD_DIM = 64


EPS = 1e-06
SCORE_SCALE = 0.015625
RESIDUAL_SCALE = 0.22
ROPE_BASE = 10000.0
NEG = -1e30


def rope_tables(positions, head_width):
    half_width = head_width // 2
    frequency = ROPE_BASE ** (-2.0 * jnp.arange(half_width, dtype=jnp.float32) / head_width)
    angles = positions.astype(jnp.float32)[:, None] * frequency[None, :]
    angles = jnp.concatenate([angles, angles], axis=1)
    return (jnp.cos(angles), jnp.sin(angles))


def apply_rotary(value_rows, cosine_table, rotary_sine_values):
    half_width = value_rows.shape[-1] // 2
    first_half = value_rows[..., :half_width]
    second_half = value_rows[..., half_width:]
    turned = jnp.concatenate([-second_half, first_half], axis=-1)
    return value_rows * cosine_table[:, None, :] + turned * rotary_sine_values[:, None, :]


def reverse_rotary(grads_in, cosine_table, rotary_sine_values):
    half_width = grads_in.shape[-1] // 2
    product = grads_in * rotary_sine_values[:, None, :]
    turned = jnp.concatenate([product[..., half_width:], -product[..., :half_width]], axis=-1)
    return grads_in * cosine_table[:, None, :] + turned


def inverse_rms(value_rows):
    return lax.rsqrt(jnp.mean(value_rows * value_rows, axis=-1, keepdims=True) + EPS)


def norm_backward(grad_normed, source, factor, gain_vector):
    scaled = grad_normed * gain_vector
    return factor * scaled - source * (factor * factor * factor) * jnp.mean(
        scaled * source, axis=-1, keepdims=True
    )


def contract_rows(left, right):
    return lax.dot_general(
        left, right, (((0,), (0,)), ((), ())), preferred_element_type=jnp.float32
    )


def contract_cols(left, right):
    return lax.dot_general(
        left, right, (((1,), (1,)), ((), ())), preferred_element_type=jnp.float32
    )


def exchange(array, axis, bit):
    size = lax.axis_size(axis)
    return lax.ppermute(array, axis, [(i, i ^ bit) for i in range(size)])


def pair_sum(part, axis):
    kept = lax.reduce_precision(part, 8, 7)
    return kept + exchange(kept.astype(jnp.bfloat16), axis, 1).astype(jnp.float32)


def axis_bits(axis):
    size = lax.axis_size(axis)
    bits = []
    bit = 1
    while bit < size:
        bits.append(bit)
        bit *= 2
    return bits


def tie(*arrays):
    return lax.optimization_barrier(arrays)


def halving_step(terms, axis, dim, bit):
    shape = terms.shape
    pairs = terms.reshape(shape[:dim] + (shape[dim] // 2, 2) + shape[dim + 1 :])
    mine = (lax.axis_index(axis) // bit) % 2
    low = lax.index_in_dim(pairs, 0, dim + 1, keepdims=False)
    high = lax.index_in_dim(pairs, 1, dim + 1, keepdims=False)
    sent = jnp.where(mine == 0, high, low).astype(jnp.bfloat16)
    kept = jnp.where(mine == 0, low, high)
    return kept.astype(jnp.float32) + exchange(sent, axis, bit).astype(jnp.float32)


def halving_sum(terms, axis, dim):
    for bit in axis_bits(axis):
        terms = halving_step(terms, axis, dim, bit)
    return lax.index_in_dim(terms, 0, dim, keepdims=False)


def ordered_step(blocks, axis, bit):
    received = exchange(blocks, axis, bit)
    mine = (lax.axis_index(axis) // bit) % 2
    low = jnp.where(mine == 0, blocks, received)
    high = jnp.where(mine == 0, received, blocks)
    return jnp.stack([low, high], axis=1).reshape((-1,) + blocks.shape[1:])


def relative_gather(block, axis):
    blocks = block[None]
    offsets = [0]
    for bit in reversed(axis_bits(axis)):
        blocks = jnp.concatenate([blocks, exchange(blocks, axis, bit)], axis=0)
        offsets = offsets + [offset ^ bit for offset in offsets]
    return blocks, offsets


def relative_sum(blocks, axis):
    for bit in axis_bits(axis):
        half = blocks.shape[0] // 2
        received = exchange(blocks[half:].astype(jnp.bfloat16), axis, bit)
        blocks = blocks[:half] + received.astype(jnp.float32)
    return blocks[0]


def body(
    inputs,
    attn_gain,
    query_weight,
    key_weight,
    value_matrix,
    output_weight,
    ffn_gain,
    gate_weight,
    up_weight,
    down_weight,
    routes,
    route_weights,
    cotangent,
):
    f32, b16 = jnp.float32, jnp.bfloat16
    shard_count = lax.axis_size("shard")
    context_count = lax.axis_size("context")
    tokens = inputs[0]
    length, model_width = tokens.shape
    rows_own = query_weight.shape[0]
    q_cols, kv_cols = query_weight.shape[1], key_weight.shape[1]
    qkv_cols = q_cols + 2 * kv_cols
    kv_heads = kv_cols // HEAD_DIM
    heads = q_cols // HEAD_DIM
    group = heads // kv_heads
    experts, hidden_units = gate_weight.shape[1], gate_weight.shape[2]
    own_experts = experts // shard_count
    own_cols = own_experts * hidden_units

    gains = jnp.pad(jnp.stack([attn_gain, ffn_gain], axis=1), ((0, 0), (0, 126)))
    packed = jnp.concatenate(
        [query_weight, key_weight, value_matrix, output_weight, gains], axis=1
    )
    packed_all = packed[None]
    for bit in reversed(axis_bits("shard")):
        packed_all = ordered_step(packed_all, "shard", bit)

    grad_out = cotangent[0]
    expert_ids = jnp.arange(experts, dtype=jnp.int32)
    dense = jnp.sum(
        jnp.where(routes[0][:, :, None] == expert_ids, route_weights[0][:, :, None], 0.0), axis=1
    )
    dense_high = lax.reduce_precision(dense, 8, 7)
    dense_low = dense - dense_high
    early = jnp.concatenate(
        [
            grad_out.astype(b16),
            dense_high.astype(b16),
            dense_low.astype(b16),
            jnp.zeros((length, 128 - 2 * experts), b16),
        ],
        axis=1,
    )

    stacked_weights = jnp.stack([gate_weight, up_weight, down_weight], axis=0)
    stacked_weights = stacked_weights.reshape(3, rows_own, shard_count, own_cols)
    stacked_weights = jnp.transpose(stacked_weights, (2, 0, 1, 3))
    owner = lax.all_to_all(stacked_weights, "shard", split_axis=0, concat_axis=0, tiled=True)
    bits = axis_bits("context")
    full = packed_all[None]
    for bit in reversed(bits[1:]):
        full = ordered_step(full, "context", bit)
    full, owner, early = tie(full, owner, early)
    full = ordered_step(full, "context", 1)
    full = jnp.swapaxes(full, 0, 1).reshape(model_width, packed.shape[1])
    qkv_full = full[:, :qkv_cols]
    output_full = full[:, qkv_cols : qkv_cols + q_cols]
    gain_rows = full[:, qkv_cols + q_cols :].astype(f32).T
    gain_attn, gain_ffn = gain_rows[0], gain_rows[1]
    early_all = early[None]
    for bit in reversed(axis_bits("shard")):
        early_all = ordered_step(early_all, "shard", bit)
    expert_blocks = owner[None]
    for bit in reversed(bits[1:]):
        expert_blocks = ordered_step(expert_blocks, "context", bit)

    context_index = lax.axis_index("context")
    positions = context_index * length + jnp.arange(length, dtype=jnp.int32)
    cosine_table, rotary_sine_values = rope_tables(positions, HEAD_DIM)
    scale_one = inverse_rms(tokens)
    normed_one = (tokens * scale_one * gain_attn).astype(b16)
    qkv_lin = jnp.dot(normed_one, qkv_full, preferred_element_type=f32)
    turned = apply_rotary(
        qkv_lin[:, : q_cols + kv_cols].reshape(length, heads + kv_heads, HEAD_DIM),
        cosine_table,
        rotary_sine_values,
    ).astype(b16)
    query_rows = turned[:, :heads].reshape(length, kv_heads, group, HEAD_DIM)
    key_rows = turned[:, heads:].reshape(length, kv_cols)
    kv_rows = jnp.concatenate([key_rows, qkv_lin[:, q_cols + kv_cols :].astype(b16)], axis=1)
    kv_blocks, offsets = relative_gather(kv_rows, "context")
    kv_all = kv_blocks.reshape(context_count * length, 2 * kv_cols)
    keys = kv_all[:, :kv_cols].reshape(-1, kv_heads, HEAD_DIM)
    values = kv_all[:, kv_cols:].reshape(-1, kv_heads, HEAD_DIM)
    owners = context_index ^ jnp.array(offsets, dtype=jnp.int32)
    key_pos = (
        owners[:, None] * length + jnp.arange(length, dtype=jnp.int32)[None, :]
    ).reshape(-1)
    visible = key_pos[None, :] <= positions[:, None]
    scores = (
        jnp.einsum("tkgd,skd->kgts", query_rows, keys, preferred_element_type=f32) * SCORE_SCALE
    )
    masked = jnp.where(visible, scores, NEG)
    weights_exp = jnp.where(visible, jnp.exp(masked - jnp.max(masked, -1, keepdims=True)), 0.0)
    soft = weights_exp / jnp.sum(weights_exp, axis=-1, keepdims=True)
    soft_b = soft.astype(b16)
    attended = jnp.einsum("kgts,skd->tkgd", soft_b, values, preferred_element_type=f32).astype(b16)
    attended_context = attended.reshape(length, q_cols)
    attn_out = pair_sum(contract_cols(attended_context, output_full), "tensor")
    hidden = tokens + RESIDUAL_SCALE * attn_out
    scale_two = inverse_rms(hidden)
    normed_two = (hidden * scale_two * gain_ffn).astype(b16)

    normed_two, expert_blocks, early_all = tie(normed_two, expert_blocks, early_all)
    early_all = early_all.reshape(shard_count * length, -1)
    expert_blocks = ordered_step(expert_blocks, "context", 1)
    expert_weights = jnp.transpose(expert_blocks, (2, 1, 0, 3, 4)).reshape(
        3, model_width, own_cols
    )
    own_gate, own_up, own_down = expert_weights[0], expert_weights[1], expert_weights[2]
    x_all = lax.all_gather(normed_two, "shard", axis=0, tiled=True)
    g_all = early_all[:, :model_width]
    dense_all = early_all[:, model_width : model_width + experts].astype(f32) + early_all[
        :, model_width + experts : model_width + 2 * experts
    ].astype(f32)
    dense_own = lax.dynamic_slice_in_dim(
        dense_all, lax.axis_index("shard") * own_experts, own_experts, 1
    )
    spread = jnp.repeat(dense_own, hidden_units, axis=1)
    grad_act = contract_dense(g_all, own_down) * (RESIDUAL_SCALE * spread)
    gate_act = contract_dense(x_all, own_gate)
    up_act = contract_dense(x_all, own_up)
    sigma = jax.nn.sigmoid(gate_act)
    swish = gate_act * sigma
    activated = (swish * up_act * spread).astype(b16)
    grad_gate = (grad_act * up_act * sigma * (1.0 + gate_act * (1.0 - sigma))).astype(b16)
    grad_up = (grad_act * swish).astype(b16)
    normed_two_terms = (contract_cols(grad_gate, own_gate) + contract_cols(grad_up, own_up)).astype(
        b16
    )
    normed_two_parts = lax.all_to_all(
        normed_two_terms.reshape(shard_count, length, model_width), "shard", 0, 0, tiled=True
    )
    moe_terms = contract_cols(activated, own_down).astype(b16)

    expert_terms = jnp.stack(
        [
            contract_rows(x_all, grad_gate),
            contract_rows(x_all, grad_up),
            RESIDUAL_SCALE * contract_rows(g_all, activated),
        ],
        axis=0,
    ).astype(b16)
    expert_terms = jnp.transpose(
        expert_terms.reshape(3, shard_count, context_count, rows_own, own_cols), (1, 2, 0, 3, 4)
    )
    expert_terms = halving_step(expert_terms, "context", 1, 1).astype(b16)
    normed_two_parts, expert_terms, moe_terms = tie(normed_two_parts, expert_terms, moe_terms)
    moe_parts = lax.all_to_all(
        moe_terms.reshape(shard_count, length, model_width), "shard", 0, 0, tiled=True
    )
    grad_normed_two = pair_sum(jnp.sum(normed_two_parts.astype(f32), axis=0), "tensor")

    term_ffn_gain = jnp.sum(grad_normed_two * hidden * scale_two, axis=0)
    grad_hidden = grad_out + norm_backward(grad_normed_two, hidden, scale_two, gain_ffn)
    grad_attn = (RESIDUAL_SCALE * grad_hidden).astype(b16)
    for bit in bits[1:]:
        expert_terms = halving_step(expert_terms, "context", 1, bit)
    context_sums = expert_terms[:, 0].astype(b16)
    context_gradient = jnp.dot(grad_attn, output_full, preferred_element_type=f32).astype(b16)
    grad_heads = context_gradient.reshape(length, kv_heads, group, HEAD_DIM)
    delta = jnp.transpose(
        jnp.sum(grad_heads.astype(f32) * attended.astype(f32), axis=-1), (1, 2, 0)
    )
    grad_soft = jnp.einsum("tkgd,skd->kgts", grad_heads, values, preferred_element_type=f32)
    grad_scores = (soft * (grad_soft - delta[..., None])).astype(b16)
    value_term = jnp.einsum("kgts,tkgd->skd", soft_b, grad_heads, preferred_element_type=f32)
    key_term = SCORE_SCALE * jnp.einsum(
        "kgts,tkgd->skd", grad_scores, query_rows, preferred_element_type=f32
    )
    kv_terms = jnp.concatenate(
        [key_term.reshape(-1, kv_cols), value_term.reshape(-1, kv_cols)], axis=1
    ).reshape(context_count, length, 2 * kv_cols)
    kv_terms, context_sums = tie(kv_terms, context_sums)
    kv_sum = relative_sum(kv_terms, "context")
    kv_sum, moe_parts = tie(kv_sum, moe_parts)
    moe = pair_sum(jnp.sum(moe_parts.astype(f32), axis=0), "tensor")
    output = hidden + RESIDUAL_SCALE * moe
    expert_sums = lax.all_to_all(context_sums, "shard", 0, 0, tiled=True)
    expert_sums = (
        jnp.transpose(expert_sums, (1, 2, 0, 3))
        .reshape(3, rows_own, experts, hidden_units)
        .astype(f32)
    )
    grad_query = SCORE_SCALE * jnp.einsum(
        "kgts,skd->tkgd", grad_scores, keys, preferred_element_type=f32
    )
    term_output = contract_rows(grad_attn, attended_context)
    turned_back = reverse_rotary(
        jnp.concatenate(
            [
                grad_query.reshape(length, heads, HEAD_DIM),
                kv_sum[:, :kv_cols].reshape(length, kv_heads, HEAD_DIM),
            ],
            axis=1,
        ),
        cosine_table,
        rotary_sine_values,
    ).reshape(length, q_cols + kv_cols)
    grad_qkv = jnp.concatenate([turned_back, kv_sum[:, kv_cols:]], axis=1).astype(b16)
    term_qkv = contract_rows(normed_one, grad_qkv)
    normed_one_part = contract_cols(grad_qkv, qkv_full)
    term_attn_gain = jnp.sum(normed_one_part * tokens * scale_one, axis=0)
    gain_terms = jnp.concatenate(
        [term_attn_gain.reshape(-1, rows_own), term_ffn_gain.reshape(-1, rows_own)], axis=1
    )
    sum_output = scatter_rows(term_output, shard_count, context_count)
    sum_rest = scatter_rows(term_qkv, shard_count, context_count)
    own_gains = scatter_rows(gain_terms, shard_count, context_count)
    grad_normed_one = pair_sum(normed_one_part, "tensor")
    grad_input = grad_hidden + norm_backward(grad_normed_one, tokens, scale_one, gain_attn)
    sum_attn_gain = (own_gains + exchange(own_gains, "tensor", 1))[0, :rows_own]
    return (
        output[None],
        grad_input[None],
        sum_attn_gain,
        sum_rest[:, :q_cols],
        sum_rest[:, q_cols : q_cols + kv_cols],
        sum_rest[:, q_cols + kv_cols : qkv_cols],
        sum_output,
        own_gains[0, rows_own:],
        expert_sums[0],
        expert_sums[1],
        expert_sums[2],
    )


def contract_dense(left, right):
    return jnp.dot(left, right, preferred_element_type=jnp.float32)


def scatter_rows(term, shard_count, context_count):
    split = term.reshape(shard_count, context_count, -1, term.shape[1])
    return halving_sum(halving_sum(split, "context", 1), "shard", 0)


def solution(mesh):
    placed = (
        P("shard", "context", None),
        P(("shard", "context")),
        P(("shard", "context"), "tensor"),
        P(("shard", "context"), "tensor"),
        P(("shard", "context"), "tensor"),
        P(("shard", "context"), "tensor"),
        P(("shard", "context")),
        P(("shard", "context"), None, "tensor"),
        P(("shard", "context"), None, "tensor"),
        P(("shard", "context"), None, "tensor"),
        P("shard", "context", None),
        P("shard", "context", None),
        P("shard", "context", None),
    )
    return jax.shard_map(
        body,
        mesh=mesh,
        in_specs=placed,
        out_specs=(
            P("shard", "context", None),
            P("shard", "context", None),
            P(("shard", "context")),
            P(("shard", "context"), "tensor"),
            P(("shard", "context"), "tensor"),
            P(("shard", "context"), "tensor"),
            P(("shard", "context"), "tensor"),
            P(("shard", "context")),
            P(("shard", "context"), None, "tensor"),
            P(("shard", "context"), None, "tensor"),
            P(("shard", "context"), None, "tensor"),
        ),
        check_vma=False,
    )
```

```python
import jax
import jax.numpy as jnp
from jax import lax
from jax.sharding import PartitionSpec as P

HEAD_DIM = 64


EPS = 1e-06
SCORE_SCALE = 0.015625
RESIDUAL_SCALE = 0.22
ROPE_BASE = 10000.0
NEG = -1e30


def rope_tables(positions, head_width):
    half_width = head_width // 2
    frequency = ROPE_BASE ** (-2.0 * jnp.arange(half_width, dtype=jnp.float32) / head_width)
    angles = positions.astype(jnp.float32)[:, None] * frequency[None, :]
    angles = jnp.concatenate([angles, angles], axis=1)
    return (jnp.cos(angles), jnp.sin(angles))


def apply_rotary(value_rows, cosine_table, rotary_sine_values):
    half_width = value_rows.shape[-1] // 2
    first_half = value_rows[..., :half_width]
    second_half = value_rows[..., half_width:]
    turned = jnp.concatenate([-second_half, first_half], axis=-1)
    return value_rows * cosine_table[:, None, :] + turned * rotary_sine_values[:, None, :]


def reverse_rotary(grads_in, cosine_table, rotary_sine_values):
    half_width = grads_in.shape[-1] // 2
    product = grads_in * rotary_sine_values[:, None, :]
    turned = jnp.concatenate([product[..., half_width:], -product[..., :half_width]], axis=-1)
    return grads_in * cosine_table[:, None, :] + turned


def inverse_rms(value_rows):
    return lax.rsqrt(jnp.mean(value_rows * value_rows, axis=-1, keepdims=True) + EPS)


def norm_backward(grad_normed, source, factor, gain_vector):
    scaled = grad_normed * gain_vector
    return factor * scaled - source * (factor * factor * factor) * jnp.mean(
        scaled * source, axis=-1, keepdims=True
    )


def contract_rows(left, right):
    return lax.dot_general(
        left, right, (((0,), (0,)), ((), ())), preferred_element_type=jnp.float32
    )


def contract_cols(left, right):
    return lax.dot_general(
        left, right, (((1,), (1,)), ((), ())), preferred_element_type=jnp.float32
    )


def exchange(array, axis, bit):
    size = lax.axis_size(axis)
    return lax.ppermute(array, axis, [(i, i ^ bit) for i in range(size)])


def pair_sum(part, axis):
    kept = lax.reduce_precision(part, 8, 7)
    return kept + exchange(kept.astype(jnp.bfloat16), axis, 1).astype(jnp.float32)


def axis_bits(axis):
    size = lax.axis_size(axis)
    bits = []
    bit = 1
    while bit < size:
        bits.append(bit)
        bit *= 2
    return bits


def tie(*arrays):
    return lax.optimization_barrier(arrays)


def halving_step(terms, axis, dim, bit):
    shape = terms.shape
    pairs = terms.reshape(shape[:dim] + (shape[dim] // 2, 2) + shape[dim + 1 :])
    mine = (lax.axis_index(axis) // bit) % 2
    low = lax.index_in_dim(pairs, 0, dim + 1, keepdims=False)
    high = lax.index_in_dim(pairs, 1, dim + 1, keepdims=False)
    sent = jnp.where(mine == 0, high, low).astype(jnp.bfloat16)
    kept = jnp.where(mine == 0, low, high)
    return kept.astype(jnp.float32) + exchange(sent, axis, bit).astype(jnp.float32)


def halving_sum(terms, axis, dim):
    for bit in axis_bits(axis):
        terms = halving_step(terms, axis, dim, bit)
    return lax.index_in_dim(terms, 0, dim, keepdims=False)


def ordered_step(blocks, axis, bit):
    received = exchange(blocks, axis, bit)
    mine = (lax.axis_index(axis) // bit) % 2
    low = jnp.where(mine == 0, blocks, received)
    high = jnp.where(mine == 0, received, blocks)
    return jnp.stack([low, high], axis=1).reshape((-1,) + blocks.shape[1:])


def relative_gather(block, axis):
    blocks = block[None]
    offsets = [0]
    for bit in reversed(axis_bits(axis)):
        blocks = jnp.concatenate([blocks, exchange(blocks, axis, bit)], axis=0)
        offsets = offsets + [offset ^ bit for offset in offsets]
    return blocks, offsets


def relative_sum(blocks, axis):
    for bit in axis_bits(axis):
        half = blocks.shape[0] // 2
        received = exchange(blocks[half:].astype(jnp.bfloat16), axis, bit)
        blocks = blocks[:half] + received.astype(jnp.float32)
    return blocks[0]


def body(
    inputs,
    attn_gain,
    query_weight,
    key_weight,
    value_matrix,
    output_weight,
    ffn_gain,
    gate_weight,
    up_weight,
    down_weight,
    routes,
    route_weights,
    cotangent,
):
    f32, b16 = jnp.float32, jnp.bfloat16
    shard_count = lax.axis_size("shard")
    context_count = lax.axis_size("context")
    tokens = inputs[0]
    length, model_width = tokens.shape
    rows_own = query_weight.shape[0]
    q_cols, kv_cols = query_weight.shape[1], key_weight.shape[1]
    qkv_cols = q_cols + 2 * kv_cols
    kv_heads = kv_cols // HEAD_DIM
    heads = q_cols // HEAD_DIM
    group = heads // kv_heads
    experts, hidden_units = gate_weight.shape[1], gate_weight.shape[2]
    own_experts = experts // shard_count
    own_cols = own_experts * hidden_units

    gains = jnp.pad(jnp.stack([attn_gain, ffn_gain], axis=1), ((0, 0), (0, 126)))
    packed = jnp.concatenate(
        [query_weight, key_weight, value_matrix, output_weight, gains], axis=1
    )
    packed_all = packed[None]
    for bit in reversed(axis_bits("shard")):
        packed_all = ordered_step(packed_all, "shard", bit)

    grad_out = cotangent[0]
    expert_ids = jnp.arange(experts, dtype=jnp.int32)
    dense = jnp.sum(
        jnp.where(routes[0][:, :, None] == expert_ids, route_weights[0][:, :, None], 0.0), axis=1
    )
    dense_high = lax.reduce_precision(dense, 8, 7)
    dense_low = dense - dense_high
    early = jnp.concatenate(
        [
            grad_out.astype(b16),
            dense_high.astype(b16),
            dense_low.astype(b16),
            jnp.zeros((length, 128 - 2 * experts), b16),
        ],
        axis=1,
    )

    stacked_weights = jnp.stack([gate_weight, up_weight, down_weight], axis=0)
    stacked_weights = stacked_weights.reshape(3, rows_own, shard_count, own_cols)
    stacked_weights = jnp.transpose(stacked_weights, (2, 0, 1, 3))
    owner = lax.all_to_all(stacked_weights, "shard", split_axis=0, concat_axis=0, tiled=True)
    bits = axis_bits("context")
    full = packed_all[None]
    for bit in reversed(bits[1:]):
        full = ordered_step(full, "context", bit)
    full = ordered_step(full, "context", 1)
    full = jnp.swapaxes(full, 0, 1).reshape(model_width, packed.shape[1])
    qkv_full = full[:, :qkv_cols]
    output_full = full[:, qkv_cols : qkv_cols + q_cols]
    gain_rows = full[:, qkv_cols + q_cols :].astype(f32).T
    gain_attn, gain_ffn = gain_rows[0], gain_rows[1]

    context_index = lax.axis_index("context")
    positions = context_index * length + jnp.arange(length, dtype=jnp.int32)
    cosine_table, rotary_sine_values = rope_tables(positions, HEAD_DIM)
    scale_one = inverse_rms(tokens)
    normed_one = (tokens * scale_one * gain_attn).astype(b16)
    qkv_lin = jnp.dot(normed_one, qkv_full, preferred_element_type=f32)
    qkv_lin, owner, early = tie(qkv_lin, owner, early)
    early_all = early[None]
    for bit in reversed(axis_bits("shard")):
        early_all = ordered_step(early_all, "shard", bit)
    expert_blocks = owner[None]
    for bit in reversed(bits[1:]):
        expert_blocks = ordered_step(expert_blocks, "context", bit)
    turned = apply_rotary(
        qkv_lin[:, : q_cols + kv_cols].reshape(length, heads + kv_heads, HEAD_DIM),
        cosine_table,
        rotary_sine_values,
    ).astype(b16)
    query_rows = turned[:, :heads].reshape(length, kv_heads, group, HEAD_DIM)
    key_rows = turned[:, heads:].reshape(length, kv_cols)
    kv_rows = jnp.concatenate([key_rows, qkv_lin[:, q_cols + kv_cols :].astype(b16)], axis=1)
    kv_blocks, offsets = relative_gather(kv_rows, "context")
    kv_all = kv_blocks.reshape(context_count * length, 2 * kv_cols)
    keys = kv_all[:, :kv_cols].reshape(-1, kv_heads, HEAD_DIM)
    values = kv_all[:, kv_cols:].reshape(-1, kv_heads, HEAD_DIM)
    owners = context_index ^ jnp.array(offsets, dtype=jnp.int32)
    key_pos = (
        owners[:, None] * length + jnp.arange(length, dtype=jnp.int32)[None, :]
    ).reshape(-1)
    visible = key_pos[None, :] <= positions[:, None]
    scores = (
        jnp.einsum("tkgd,skd->kgts", query_rows, keys, preferred_element_type=f32) * SCORE_SCALE
    )
    masked = jnp.where(visible, scores, NEG)
    weights_exp = jnp.where(visible, jnp.exp(masked - jnp.max(masked, -1, keepdims=True)), 0.0)
    soft = weights_exp / jnp.sum(weights_exp, axis=-1, keepdims=True)
    soft_b = soft.astype(b16)
    attended = jnp.einsum("kgts,skd->tkgd", soft_b, values, preferred_element_type=f32).astype(b16)
    attended_context = attended.reshape(length, q_cols)
    attn_out = pair_sum(contract_cols(attended_context, output_full), "tensor")
    hidden = tokens + RESIDUAL_SCALE * attn_out
    scale_two = inverse_rms(hidden)
    normed_two = (hidden * scale_two * gain_ffn).astype(b16)

    normed_two, expert_blocks, early_all = tie(normed_two, expert_blocks, early_all)
    early_all = early_all.reshape(shard_count * length, -1)
    expert_blocks = ordered_step(expert_blocks, "context", 1)
    expert_weights = jnp.transpose(expert_blocks, (2, 1, 0, 3, 4)).reshape(
        3, model_width, own_cols
    )
    own_gate, own_up, own_down = expert_weights[0], expert_weights[1], expert_weights[2]
    x_all = lax.all_gather(normed_two, "shard", axis=0, tiled=True)
    g_all = early_all[:, :model_width]
    dense_all = early_all[:, model_width : model_width + experts].astype(f32) + early_all[
        :, model_width + experts : model_width + 2 * experts
    ].astype(f32)
    dense_own = lax.dynamic_slice_in_dim(
        dense_all, lax.axis_index("shard") * own_experts, own_experts, 1
    )
    spread = jnp.repeat(dense_own, hidden_units, axis=1)
    grad_act = contract_dense(g_all, own_down) * (RESIDUAL_SCALE * spread)
    gate_act = contract_dense(x_all, own_gate)
    up_act = contract_dense(x_all, own_up)
    sigma = jax.nn.sigmoid(gate_act)
    swish = gate_act * sigma
    activated = (swish * up_act * spread).astype(b16)
    grad_gate = (grad_act * up_act * sigma * (1.0 + gate_act * (1.0 - sigma))).astype(b16)
    grad_up = (grad_act * swish).astype(b16)
    normed_two_terms = (contract_cols(grad_gate, own_gate) + contract_cols(grad_up, own_up)).astype(
        b16
    )
    normed_two_parts = lax.all_to_all(
        normed_two_terms.reshape(shard_count, length, model_width), "shard", 0, 0, tiled=True
    )
    moe_terms = contract_cols(activated, own_down).astype(b16)

    expert_terms = jnp.stack(
        [
            contract_rows(x_all, grad_gate),
            contract_rows(x_all, grad_up),
            RESIDUAL_SCALE * contract_rows(g_all, activated),
        ],
        axis=0,
    ).astype(b16)
    expert_terms = jnp.transpose(
        expert_terms.reshape(3, shard_count, context_count, rows_own, own_cols), (1, 2, 0, 3, 4)
    )
    expert_terms = halving_step(expert_terms, "context", 1, 1).astype(b16)
    normed_two_parts, expert_terms, moe_terms = tie(normed_two_parts, expert_terms, moe_terms)
    moe_parts = lax.all_to_all(
        moe_terms.reshape(shard_count, length, model_width), "shard", 0, 0, tiled=True
    )
    grad_normed_two = pair_sum(jnp.sum(normed_two_parts.astype(f32), axis=0), "tensor")

    term_ffn_gain = jnp.sum(grad_normed_two * hidden * scale_two, axis=0)
    grad_hidden = grad_out + norm_backward(grad_normed_two, hidden, scale_two, gain_ffn)
    grad_attn = (RESIDUAL_SCALE * grad_hidden).astype(b16)
    for bit in bits[1:]:
        expert_terms = halving_step(expert_terms, "context", 1, bit)
    context_sums = expert_terms[:, 0].astype(b16)
    context_gradient = jnp.dot(grad_attn, output_full, preferred_element_type=f32).astype(b16)
    grad_heads = context_gradient.reshape(length, kv_heads, group, HEAD_DIM)
    delta = jnp.transpose(
        jnp.sum(grad_heads.astype(f32) * attended.astype(f32), axis=-1), (1, 2, 0)
    )
    grad_soft = jnp.einsum("tkgd,skd->kgts", grad_heads, values, preferred_element_type=f32)
    grad_scores = (soft * (grad_soft - delta[..., None])).astype(b16)
    value_term = jnp.einsum("kgts,tkgd->skd", soft_b, grad_heads, preferred_element_type=f32)
    key_term = SCORE_SCALE * jnp.einsum(
        "kgts,tkgd->skd", grad_scores, query_rows, preferred_element_type=f32
    )
    kv_terms = jnp.concatenate(
        [key_term.reshape(-1, kv_cols), value_term.reshape(-1, kv_cols)], axis=1
    ).reshape(context_count, length, 2 * kv_cols)
    kv_terms, context_sums = tie(kv_terms, context_sums)
    kv_sum = relative_sum(kv_terms, "context")
    kv_sum, moe_parts = tie(kv_sum, moe_parts)
    moe = pair_sum(jnp.sum(moe_parts.astype(f32), axis=0), "tensor")
    output = hidden + RESIDUAL_SCALE * moe
    expert_sums = lax.all_to_all(context_sums, "shard", 0, 0, tiled=True)
    expert_sums = (
        jnp.transpose(expert_sums, (1, 2, 0, 3))
        .reshape(3, rows_own, experts, hidden_units)
        .astype(f32)
    )
    grad_query = SCORE_SCALE * jnp.einsum(
        "kgts,skd->tkgd", grad_scores, keys, preferred_element_type=f32
    )
    term_output = contract_rows(grad_attn, attended_context)
    turned_back = reverse_rotary(
        jnp.concatenate(
            [
                grad_query.reshape(length, heads, HEAD_DIM),
                kv_sum[:, :kv_cols].reshape(length, kv_heads, HEAD_DIM),
            ],
            axis=1,
        ),
        cosine_table,
        rotary_sine_values,
    ).reshape(length, q_cols + kv_cols)
    grad_qkv = jnp.concatenate([turned_back, kv_sum[:, kv_cols:]], axis=1).astype(b16)
    term_qkv = contract_rows(normed_one, grad_qkv)
    normed_one_part = contract_cols(grad_qkv, qkv_full)
    term_attn_gain = jnp.sum(normed_one_part * tokens * scale_one, axis=0)
    gain_terms = jnp.concatenate(
        [term_attn_gain.reshape(-1, rows_own), term_ffn_gain.reshape(-1, rows_own)], axis=1
    )
    sum_output = scatter_rows(term_output, shard_count, context_count)
    sum_rest = scatter_rows(term_qkv, shard_count, context_count)
    own_gains = scatter_rows(gain_terms, shard_count, context_count)
    grad_normed_one = pair_sum(normed_one_part, "tensor")
    grad_input = grad_hidden + norm_backward(grad_normed_one, tokens, scale_one, gain_attn)
    sum_attn_gain = (own_gains + exchange(own_gains, "tensor", 1))[0, :rows_own]
    return (
        output[None],
        grad_input[None],
        sum_attn_gain,
        sum_rest[:, :q_cols],
        sum_rest[:, q_cols : q_cols + kv_cols],
        sum_rest[:, q_cols + kv_cols : qkv_cols],
        sum_output,
        own_gains[0, rows_own:],
        expert_sums[0],
        expert_sums[1],
        expert_sums[2],
    )


def contract_dense(left, right):
    return jnp.dot(left, right, preferred_element_type=jnp.float32)


def scatter_rows(term, shard_count, context_count):
    split = term.reshape(shard_count, context_count, -1, term.shape[1])
    return halving_sum(halving_sum(split, "context", 1), "shard", 0)


def solution(mesh):
    placed = (
        P("shard", "context", None),
        P(("shard", "context")),
        P(("shard", "context"), "tensor"),
        P(("shard", "context"), "tensor"),
        P(("shard", "context"), "tensor"),
        P(("shard", "context"), "tensor"),
        P(("shard", "context")),
        P(("shard", "context"), None, "tensor"),
        P(("shard", "context"), None, "tensor"),
        P(("shard", "context"), None, "tensor"),
        P("shard", "context", None),
        P("shard", "context", None),
        P("shard", "context", None),
    )
    return jax.shard_map(
        body,
        mesh=mesh,
        in_specs=placed,
        out_specs=(
            P("shard", "context", None),
            P("shard", "context", None),
            P(("shard", "context")),
            P(("shard", "context"), "tensor"),
            P(("shard", "context"), "tensor"),
            P(("shard", "context"), "tensor"),
            P(("shard", "context"), "tensor"),
            P(("shard", "context")),
            P(("shard", "context"), None, "tensor"),
            P(("shard", "context"), None, "tensor"),
            P(("shard", "context"), None, "tensor"),
        ),
        check_vma=False,
    )
```
